32 devices in a mesh: ctx: 16 (over z, y, core), fsdp: 2 (over x).
Axes of the slice: x: 2, y: 2, z: 4, core: 2. Of those that a mesh axis runs over, the one named last changes fastest.
Arguments:
- tokens: bfloat16 [2, 4096, 768], P('fsdp', 'ctx')
- segments: int32 [2, 4096], P('fsdp', 'ctx'), may hold values from 0 to 6, as said below
- cotangent: bfloat16 [2, 4096, 768], P('fsdp', 'ctx'), may hold values from -6 to 6
- ln1_gain: bfloat16 [768], P('fsdp'), may hold values from 0.5 to 1.5
- ln1_bias: bfloat16 [768], P('fsdp'), may hold values from -4 to 4
- qkv_weight: bfloat16 [768, 2304], P('fsdp'), may hold values from -0.21875 to 0.21875
- q_bias: bfloat16 [768], P('fsdp'), may hold values from -4 to 4
- v_bias: bfloat16 [768], P('fsdp'), may hold values from -4 to 4
- out_weight: bfloat16 [768, 768], P('fsdp'), may hold values from -0.21875 to 0.21875
- out_bias: bfloat16 [768], P('fsdp'), may hold values from -4 to 4
- ln2_gain: bfloat16 [768], P('fsdp'), may hold values from 0.5 to 1.5
- ln2_bias: bfloat16 [768], P('fsdp'), may hold values from -4 to 4
- up_weight: bfloat16 [768, 3072], P('fsdp')
- up_bias: bfloat16 [3072], P('fsdp'), may hold values from -4 to 4
- down_weight: bfloat16 [3072, 768], P('fsdp'), may hold values from -0.109375 to 0.109375
- down_bias: bfloat16 [768], P('fsdp'), may hold values from -4 to 4
Outputs:
- layer_out: bfloat16 [2, 4096, 768], P('fsdp', 'ctx')
- input_grad: bfloat16 [2, 4096, 768], P('fsdp', 'ctx')
- ln1_gain_grad: float32 [768], P('fsdp')
- ln1_bias_grad: float32 [768], P('fsdp')
- qkv_weight_grad: float32 [768, 2304], P('fsdp')
- q_bias_grad: float32 [768], P('fsdp')
- v_bias_grad: float32 [768], P('fsdp')
- out_weight_grad: float32 [768, 768], P('fsdp')
- out_bias_grad: float32 [768], P('fsdp')
- ln2_gain_grad: float32 [768], P('fsdp')
- ln2_bias_grad: float32 [768], P('fsdp')
- up_weight_grad: float32 [768, 3072], P('fsdp')
- up_bias_grad: float32 [3072], P('fsdp')
- down_weight_grad: float32 [3072, 768], P('fsdp')
- down_bias_grad: float32 [768], P('fsdp')
- stream_rms: float32 [3], replicated
The draws below stay inside these ranges and needn't reach their ends.
Inputs may be any that keep to these rules, and one draw needn't show every extreme that they name: `segments`: the nonzero segment numbers never fall along a sequence; runs of padding (0) may stand between or inside documents and at a sequence's end. One document of each sequence has tokens within its first 256 tokens and within its last 256.
All inputs are finite; a program needn't handle non-finite values.
Results may differ from the reference program's by a relative error of at most 0.019.
Values may be sent and summed in bfloat16 or wider, within the bound.
No kernel may reach another device: no remote copies, remote signals or barrier semaphores. Data moves between devices by JAX's collectives and lax.ppermute only.
A program may use at most 128 MiB of HBM per device.

```python
import math
import jax
import jax.numpy as jnp
from jax import lax

D = 768
HEADS = 12
HEAD_DIM = 64
FF = 3072
TOK_DEV = 256
SEQS = 2
LEN = 4096


def draw_tokens(key, part):
    where = jnp.arange(LEN, dtype=jnp.float32) / LEN
    rising = (0.5 + where)[None, :, None]
    base = jnp.clip(jax.random.normal(key, (SEQS, LEN, D), jnp.float32), -6.0, 6.0)
    return (base * rising).astype(jnp.bfloat16)


def draw_segments(key, part):
    head_key = jax.random.fold_in(key, 11)
    tail_key = jax.random.fold_in(key, 12)
    pad_key = jax.random.fold_in(key, 13)
    hole_key = jax.random.fold_in(key, 14)
    blocks = LEN // TOK_DEV
    head_len = jax.random.randint(head_key, (SEQS, 1), TOK_DEV // 4, TOK_DEV // 2)
    tail_len = jax.random.randint(tail_key, (SEQS, 1), TOK_DEV // 4, TOK_DEV // 2)
    pad_len = jax.random.randint(pad_key, (SEQS, 1), TOK_DEV // 8, TOK_DEV // 4 + 1)
    holes = jax.random.randint(hole_key, (SEQS, blocks), 0, 3 * TOK_DEV // 4 + 1)
    position = jnp.arange(LEN, dtype=jnp.int32)[None, :]
    block_of = position // TOK_DEV
    in_block = position % TOK_DEV
    hole_here = jnp.repeat(holes, TOK_DEV, axis=1)
    inner = (block_of > 0) & (block_of < blocks - 1) & (in_block >= TOK_DEV - hole_here)
    tail_start = LEN - pad_len - tail_len
    first_docs = 1 + position * 3 // head_len
    last_docs = 5 + (position - tail_start) * 2 // tail_len
    seg_ids = jnp.where(position < head_len, first_docs, 4)
    seg_ids = jnp.where(position >= tail_start, last_docs, seg_ids)
    seg_ids = jnp.where(position >= LEN - pad_len, 0, seg_ids)
    seg_ids = jnp.where(inner, 0, seg_ids)
    return seg_ids.astype(jnp.int32)


def draw_up_weight(key, part):
    key = jax.random.fold_in(key, 21)
    column_key = jax.random.fold_in(key, 22)
    scale = D ** (-0.5)
    offset = 0.5 * jnp.clip(jax.random.normal(column_key, (1, FF), jnp.float32), -4.0, 4.0)
    base = jnp.clip(jax.random.normal(key, (D, FF), jnp.float32), -4.0, 4.0)
    return ((base + offset) * scale).astype(jnp.bfloat16)


def level_of(stream_key, extent, shards, least, top_value):
    def one(dim, shards_of):
        draws = jax.random.uniform(jax.random.fold_in(jax.random.fold_in(stream_key, 6), dim), (shards_of,), jnp.float32, least / len(shards), top_value / len(shards))
        return jnp.repeat(jnp.exp(draws), extent[dim] // shards_of).reshape((-1,) + (1,) * (len(extent) - dim - 1))

    factor_of = one(*shards[0])
    for cut in shards[1:]:
        factor_of = factor_of * one(*cut)
    return factor_of


def normal_values(stream_key, dims, spread, reach, pieces=(), held_as=jnp.bfloat16):
    values = jax.random.normal(stream_key, dims, jnp.float32) * spread
    if len(pieces) > 0:
        values = level_of(stream_key, dims, pieces, -0.22, 0.18) * values
    return jnp.clip(values, min=-reach, max=reach).astype(held_as)


def setup_inputs(seed: int = 0) -> dict:
    seeds = jax.random.split(jax.random.key(seed), 17)
    return {
        "tokens": draw_tokens(jax.random.fold_in(seeds[16], 71), 0),
        "segments": draw_segments(jax.random.fold_in(seeds[16], 71), 0),
        "cotangent": normal_values(seeds[2], (SEQS, LEN, D), 1.0, 6.0, ((0, 2), (1, 16))),
        "ln1_gain": jnp.clip(1.0 + 0.1 * jax.random.normal(seeds[3], (D,), jnp.float32), 0.5, 1.5).astype(jnp.bfloat16),
        "ln1_bias": normal_values(seeds[4], (D,), 0.3, 4.0, ((0, 2),)),
        "qkv_weight": normal_values(seeds[5], (D, 3 * D), D ** -0.5, 0.21875, ((0, 2),)),
        "q_bias": normal_values(seeds[6], (D,), 0.3, 4.0, ((0, 2),)),
        "v_bias": normal_values(seeds[7], (D,), 0.5, 4.0, ((0, 2),)),
        "out_weight": normal_values(seeds[8], (D, D), D ** -0.5, 0.21875, ((0, 2),)),
        "out_bias": normal_values(seeds[9], (D,), 0.3, 4.0, ((0, 2),)),
        "ln2_gain": jnp.clip(1.0 + 0.1 * jax.random.normal(seeds[10], (D,), jnp.float32), 0.5, 1.5).astype(jnp.bfloat16),
        "ln2_bias": normal_values(seeds[11], (D,), 0.3, 4.0, ((0, 2),)),
        "up_weight": draw_up_weight(jax.random.fold_in(seeds[16], 71), 0),
        "up_bias": normal_values(seeds[13], (FF,), 0.5, 4.0, ((0, 2),)),
        "down_weight": normal_values(seeds[14], (FF, D), FF ** -0.5, 0.109375, ((0, 2),)),
        "down_bias": normal_values(seeds[15], (D,), 0.3, 4.0, ((0, 2),)),
    }


EPS = 1e-06
NEG = -1000000000.0

@jax.custom_vjp
def low(v):
    return lax.optimization_barrier(v.astype(jnp.bfloat16)).astype(jnp.float32)

@jax.custom_vjp
def low_back(v):
    return v

def low_keep(v):
    return (low(v), None)

def low_pass(kept, grad):
    return (grad,)

def back_keep(v):
    return (v, None)

def back_low(kept, grad):
    return (low(grad),)
low.defvjp(low_keep, low_pass)
low_back.defvjp(back_keep, back_low)

def layer_norm(inputs, gain_vec, bias_vec):
    row_mean = lax.optimization_barrier(jnp.mean(inputs, axis=-1, keepdims=True))
    centred = inputs - row_mean
    variance = lax.optimization_barrier(jnp.mean(centred * centred, axis=-1, keepdims=True))
    return centred * lax.rsqrt(variance + EPS) * gain_vec + bias_vec

def product(left, right):
    return jnp.dot(left, right, precision=lax.Precision.HIGHEST)

def attention(queries, keys, values, seg_row):
    length = queries.shape[0]
    block_rows = math.gcd(512, length)
    score_scale = queries.shape[2] ** (-0.5)
    query_blocks = queries.reshape(length // block_rows, block_rows, queries.shape[1], queries.shape[2])
    seg_blocks = seg_row.reshape(length // block_rows, block_rows)

    def attend_rows(block_args):
        query_block, query_seg = block_args
        scores = low_back(jnp.einsum('qhd,khd->hqk', query_block, keys, precision=lax.Precision.HIGHEST) * score_scale)
        same_doc = (query_seg[:, None] == seg_row[None, :])[None]
        scores = jnp.where(same_doc, scores, NEG)
        row_max = lax.optimization_barrier(jnp.max(scores, axis=-1, keepdims=True))
        expo = jnp.where(same_doc, jnp.exp(scores - row_max), 0.0)
        probs = low(expo / lax.optimization_barrier(jnp.sum(expo, axis=-1, keepdims=True)))
        return jnp.einsum('hqk,khd->qhd', probs, values, precision=lax.Precision.HIGHEST)
    result = lax.map(jax.checkpoint(attend_rows), (query_blocks, seg_blocks))
    return result.reshape(length, queries.shape[1] * queries.shape[2])

def block_layer(layer_in, seg_row, params):
    gain_one, shift_one, w_qkv, bias_query, bias_value, w_out, bias_out, gain_two, shift_two, w_up, bias_up, w_down, bias_down = params
    length = layer_in.shape[0]
    normed = low(layer_norm(layer_in, gain_one, shift_one))
    qkv_bias = jnp.concatenate([bias_query, jnp.zeros_like(bias_query), bias_value])
    qkv = low(low_back(product(normed, w_qkv)) + qkv_bias)
    split_heads = qkv.reshape(length, 3, HEADS, HEAD_DIM)
    attn = low(low_back(attention(split_heads[:, 0], split_heads[:, 1], split_heads[:, 2], seg_row)))
    mid_stream = layer_in + low_back(product(attn, w_out)) + bias_out
    normed_two = low(layer_norm(mid_stream, gain_two, shift_two))
    up_pre = low_back(product(normed_two, w_up)) + bias_up
    hidden = low(jax.nn.gelu(up_pre, approximate=True))
    out_stream = mid_stream + product(hidden, w_down) + bias_down
    return (out_stream, mid_stream)

def reference(tokens, segments, cotangent, ln1_gain, ln1_bias, qkv_weight, q_bias, v_bias, out_weight, out_bias, ln2_gain, ln2_bias, up_weight, up_bias, down_weight, down_bias):
    params = tuple((a.astype(jnp.float32) for a in (ln1_gain, ln1_bias, qkv_weight, q_bias, v_bias, out_weight, out_bias, ln2_gain, ln2_bias, up_weight, up_bias, down_weight, down_bias)))
    inputs = tokens.astype(jnp.float32)

    def run_layer(stream_in, layer_params):

        def one_sequence(state_now, member):
            out_stream, mid_stream = block_layer(member[0], member[1], layer_params)
            return (state_now, (out_stream, mid_stream))
        _, (outs_all, mids_all) = lax.scan(one_sequence, jnp.zeros((), jnp.float32), (stream_in, segments))
        return (outs_all, mids_all)
    outs_all, back_fn, mids_all = jax.vjp(run_layer, inputs, params, has_aux=True)
    grad_in, grads = back_fn(cotangent.astype(jnp.float32))
    valid = (segments > 0).astype(jnp.float32)[..., None]
    counted = jnp.sum(valid) * inputs.shape[2]
    squares = jnp.stack([jnp.sum(valid * inputs * inputs), jnp.sum(valid * mids_all * mids_all), jnp.sum(valid * outs_all * outs_all)])
    stream_rms = jnp.sqrt(squares / counted)
    return (outs_all.astype(jnp.bfloat16), grad_in.astype(jnp.bfloat16), grads[0], grads[1], grads[2], grads[3], grads[4], grads[5], grads[6], grads[7], grads[8], grads[9], grads[10], grads[11], grads[12], stream_rms)
```

```python
import math

import jax
import jax.numpy as jnp
from jax import lax
from jax.experimental import pallas as pl
from jax.experimental.pallas import tpu as pltpu
from jax.sharding import PartitionSpec as P

D = 768
HEADS = 12
HEAD_DIM = 64
FF = 3072
EPS = 1e-06
GROUPS = 4
GH = HEADS // GROUPS
GW = GH * HEAD_DIM
FAR = -(2.0**100)
LOG2E = math.log2(math.e)
BF = jnp.bfloat16
F32 = jnp.float32


def swap(block, axis, mask):
    size = lax.axis_size(axis)
    return lax.ppermute(block, axis, [(i, i ^ mask) for i in range(size)])


def gather(blocks, axis, masks):
    for mask in masks:
        blocks = jnp.concatenate([blocks, swap(blocks, axis, mask)], axis=0)
    return blocks


def reduce_blocks(blocks, axis, masks):
    for mask in reversed(masks):
        half = blocks.shape[0] // 2
        got = swap(blocks[half:], axis, mask)
        blocks = (blocks[:half].astype(F32) + got.astype(F32)).astype(BF)
    return blocks


def orders(masks):
    out = [0]
    for mask in masks:
        out = out + [d ^ mask for d in out]
    return out


def arranged(blocks, distances, me, unit=1):
    n = len(distances)
    if n == 2:
        return jnp.where(me == 0, blocks, blocks[::-1])
    place = [distances.index(d * unit) for d in range(n)]
    table = jnp.array(place, jnp.int32)
    return jnp.stack(
        [lax.dynamic_index_in_dim(blocks, table[a ^ me], 0, keepdims=False) for a in range(n)]
    )


def rows_product(left, right):
    return lax.dot_general(
        left, right, (((0,), (0,)), ((), ())), preferred_element_type=F32
    )


def cols_product(left, right):
    return lax.dot_general(
        left, right, (((1,), (1,)), ((), ())), preferred_element_type=F32
    )


def standard(inputs):
    row_mean = jnp.mean(inputs, axis=-1, keepdims=True)
    centred = inputs - row_mean
    variance = jnp.mean(centred * centred, axis=-1, keepdims=True)
    scale = lax.rsqrt(variance + EPS)
    return centred * scale, scale


def standard_back(grad, unit, scale):
    return scale * (
        grad
        - jnp.mean(grad, axis=-1, keepdims=True)
        - unit * jnp.mean(grad * unit, axis=-1, keepdims=True)
    )


def gelu_tanh(inputs):
    return jax.nn.gelu(inputs, approximate=True)


def three_parts(value):
    top = value.astype(BF).astype(F32)
    rest = value - top
    middle = rest.astype(BF).astype(F32)
    return top, middle, rest - middle


def query_side(head_t, extra):
    return jnp.concatenate([head_t, extra.astype(BF)], axis=0)


def forward_kernel(tiles, q_ref, k_ref, v_ref, mark_ref, seg_ref, ft_ref, low_ref, log_ref, q_s, m_s, acc_s):
    step = pl.program_id(0)
    n_q = q_ref.shape[0]

    @pl.when(step == 0)
    def _():
        q_t = q_ref[...].T
        row = lax.broadcasted_iota(jnp.int32, (HEAD_DIM, n_q), 0)
        away = (row < 8) & (row.astype(F32) != seg_ref[...])
        extra = jnp.where(away, FAR, 0.0)
        for h in range(GH):
            q_s[h] = query_side(q_t[h * HEAD_DIM : (h + 1) * HEAD_DIM], extra)
        m_s[...] = jnp.full_like(m_s, 2 * FAR)
        acc_s[...] = jnp.zeros_like(acc_s)

    v_t = v_ref[...].T
    ones = jnp.ones((16, v_t.shape[1]), BF)
    for h in range(GH):
        mine = slice(h * HEAD_DIM, (h + 1) * HEAD_DIM)
        keys = jnp.concatenate([k_ref[:, mine], mark_ref[...]], axis=1)
        scores = jnp.dot(keys, q_s[h], preferred_element_type=F32)
        old = m_s[h]
        new = jnp.maximum(old, jnp.max(scores, axis=0, keepdims=True))
        weights = jnp.exp2(scores - new)
        m_s[h] = new
        values = jnp.concatenate([v_t[mine], ones], axis=0)
        acc_s[h] = acc_s[h] * jnp.exp2(old - new) + jnp.dot(
            values, weights.astype(BF), preferred_element_type=F32
        )

    @pl.when(step == pl.num_programs(0) - 1)
    def _():
        parts = []
        for h in range(GH):
            total = acc_s[h, HEAD_DIM : HEAD_DIM + 1]
            parts.append(acc_s[h, :HEAD_DIM] / total)
            log_ref[h] = m_s[h] + jnp.log2(total)
        whole = jnp.concatenate(parts, axis=0)
        ft_ref[...] = whole
        low_ref[...] = whole.astype(BF).T


def forward_attention(q, k, v, mark, seg_row):
    n_q, n_k = q.shape[0], k.shape[0]
    block = 1024
    return pl.pallas_call(
        lambda *refs: forward_kernel(n_k // block, *refs),
        name="attention_forward",
        grid=(n_k // block,),
        in_specs=[
            pl.BlockSpec((n_q, GW), lambda i: (0, 0)),
            pl.BlockSpec((block, GW), lambda i: (i, 0)),
            pl.BlockSpec((block, GW), lambda i: (i, 0)),
            pl.BlockSpec((block, HEAD_DIM), lambda i: (i, 0)),
            pl.BlockSpec((1, n_q), lambda i: (0, 0)),
        ],
        out_specs=[
            pl.BlockSpec((GW, n_q), lambda i: (0, 0)),
            pl.BlockSpec((n_q, GW), lambda i: (0, 0)),
            pl.BlockSpec((GH, 1, n_q), lambda i: (0, 0, 0)),
        ],
        out_shape=[
            jax.ShapeDtypeStruct((GW, n_q), F32),
            jax.ShapeDtypeStruct((n_q, GW), BF),
            jax.ShapeDtypeStruct((GH, 1, n_q), F32),
        ],
        scratch_shapes=[
            pltpu.VMEM((GH, 2 * HEAD_DIM, n_q), BF),
            pltpu.VMEM((GH, 1, n_q), F32),
            pltpu.VMEM((GH, HEAD_DIM + 16, n_q), F32),
        ],
        compiler_params=pltpu.CompilerParams(vmem_limit_bytes=30 * 1024 * 1024),
        cost_estimate=pl.CostEstimate(
            flops=4 * n_q * n_k * 256 * GH, bytes_accessed=8 << 20, transcendentals=GH * n_q * n_k
        ),
    )(q, k, v, mark, seg_row)


def backward_kernel(
    q_ref, g_ref, ft_ref, log_ref, seg_ref, k_ref, v_ref, mark_ref,
    dq_ref, dk_ref, dv_ref, sum_ref, q_s, g_s, dq_s,
):
    step = pl.program_id(0)
    n_q = q_ref.shape[0]

    @pl.when(step == 0)
    def _():
        q_t = q_ref[...].T
        g_t = g_ref[...].T
        row = lax.broadcasted_iota(jnp.int32, (HEAD_DIM, n_q), 0)
        away = jnp.where((row < 8) & (row.astype(F32) != seg_ref[...]), FAR, 0.0)

        def with_parts(base, value):
            top, middle, low = three_parts(value)
            base = jnp.where(row == 8, -top, base)
            base = jnp.where(row == 9, -middle, base)
            return jnp.where(row == 10, -low, base)

        for h in range(GH):
            mine = slice(h * HEAD_DIM, (h + 1) * HEAD_DIM)
            q_s[h] = query_side(q_t[mine], with_parts(away, log_ref[h]))
            delta = jnp.sum(g_t[mine].astype(F32) * ft_ref[mine], axis=0, keepdims=True)
            g_s[h] = query_side(g_t[mine], with_parts(jnp.zeros_like(away), delta))
        dq_s[...] = jnp.zeros_like(dq_s)

    k_t = k_ref[...].T
    dks, dvs = [], []
    for h in range(GH):
        mine = slice(h * HEAD_DIM, (h + 1) * HEAD_DIM)
        keys = jnp.concatenate([k_ref[:, mine], mark_ref[...]], axis=1)
        values = jnp.concatenate([v_ref[:, mine], mark_ref[...]], axis=1)
        probs = jnp.exp2(jnp.dot(keys, q_s[h], preferred_element_type=F32))
        d_probs = jnp.dot(values, g_s[h], preferred_element_type=F32)
        d_scores = (probs * d_probs).astype(BF)
        dvs.append(jnp.dot(probs.astype(BF), g_ref[:, mine], preferred_element_type=F32))
        dks.append(jnp.dot(d_scores, q_ref[:, mine], preferred_element_type=F32))
        dq_s[mine] += jnp.dot(k_t[mine], d_scores, preferred_element_type=F32)
    dk_ref[...] = (jnp.concatenate(dks, axis=1) * (1.0 / LOG2E)).astype(BF)
    dv_ref[...] = jnp.concatenate(dvs, axis=1).astype(BF)

    @pl.when(step == pl.num_programs(0) - 1)
    def _():
        dq = dq_s[...].T * (HEAD_DIM**-0.5)
        dq_ref[...] = dq.astype(BF)
        sum_ref[...] = jnp.sum(dq, axis=0, keepdims=True)


def backward_attention(q, g, ft, log, seg_row, k, v, mark):
    n_q, n_k = q.shape[0], k.shape[0]
    block = 512
    whole = lambda i: (0, 0)
    part = lambda i: (i, 0)
    return pl.pallas_call(
        backward_kernel,
        name="attention_backward",
        grid=(n_k // block,),
        in_specs=[
            pl.BlockSpec((n_q, GW), whole),
            pl.BlockSpec((n_q, GW), whole),
            pl.BlockSpec((GW, n_q), whole),
            pl.BlockSpec((GH, 1, n_q), lambda i: (0, 0, 0)),
            pl.BlockSpec((1, n_q), whole),
            pl.BlockSpec((block, GW), part),
            pl.BlockSpec((block, GW), part),
            pl.BlockSpec((block, HEAD_DIM), part),
        ],
        out_specs=[
            pl.BlockSpec((n_q, GW), whole),
            pl.BlockSpec((block, GW), part),
            pl.BlockSpec((block, GW), part),
            pl.BlockSpec((1, GW), whole),
        ],
        out_shape=[
            jax.ShapeDtypeStruct((n_q, GW), BF),
            jax.ShapeDtypeStruct((n_k, GW), BF),
            jax.ShapeDtypeStruct((n_k, GW), BF),
            jax.ShapeDtypeStruct((1, GW), F32),
        ],
        scratch_shapes=[
            pltpu.VMEM((GH, 2 * HEAD_DIM, n_q), BF),
            pltpu.VMEM((GH, 2 * HEAD_DIM, n_q), BF),
            pltpu.VMEM((GW, n_q), F32),
        ],
        compiler_params=pltpu.CompilerParams(vmem_limit_bytes=30 * 1024 * 1024),
        cost_estimate=pl.CostEstimate(
            flops=10 * n_q * n_k * 256 * GH, bytes_accessed=12 << 20, transcendentals=GH * n_q * n_k
        ),
    )(q, g, ft, log, seg_row, k, v, mark)


def body(
    tokens,
    segments,
    cotangent,
    ln1_gain,
    ln1_bias,
    qkv_weight,
    q_bias,
    v_bias,
    out_weight,
    out_bias,
    ln2_gain,
    ln2_bias,
    up_weight,
    up_bias,
    down_weight,
    down_bias,
):
    n_ctx, n_f = lax.axis_size("ctx"), lax.axis_size("fsdp")
    ring = n_ctx // GROUPS
    rows = tokens.shape[1]
    ctx, xi = lax.axis_index("ctx"), lax.axis_index("fsdp")
    zi, core = ctx // ring, ctx % 2
    f_masks = [1 << b for b in range(n_f.bit_length() - 1)]
    y_masks = [1 << b for b in range(1, ring.bit_length() - 1)]
    z_masks = [ring, 2 * ring]
    r_masks = y_masks + [1]
    f_order = orders(f_masks)

    all_seg = lax.all_gather(segments, "ctx", axis=1, tiled=True)[0]
    sent = tokens[0]
    z_blocks = [sent] + [swap(sent, "ctx", k * ring) for k in range(1, GROUPS)]
    row_tokens = jnp.concatenate(z_blocks, axis=0)

    def segs_of(distance):
        return lax.dynamic_slice_in_dim(all_seg, (ctx ^ distance) * rows, rows)

    own_cols = jnp.concatenate(
        [lax.dynamic_slice_in_dim(qkv_weight, p * D + zi * GW, GW, axis=1) for p in range(3)],
        axis=1,
    )
    small = jnp.concatenate(
        [ln1_gain, ln1_bias, q_bias, v_bias, out_bias, ln2_gain, ln2_bias, down_bias, up_bias]
    )
    small = jnp.pad(small.reshape(-1, 3 * GW), ((0, 16 - 16 // n_f), (0, 0)))
    first = jnp.concatenate([own_cols, small], axis=0)[None]
    first = lax.all_gather(first[0], "fsdp")
    share = D // n_f
    w_own = first[:, :share].reshape(D, 3 * GW)
    vectors = first[:, share : share + 16 // n_f].reshape(n_f, -1)

    def vector(i, width=share):
        return vectors[:, i * share : i * share + width].reshape(-1).astype(F32)

    gain_one, shift_one, bias_query, bias_value = (vector(i) for i in range(4))
    bias_out, gain_two, shift_two, bias_down = (vector(i) for i in range(4, 8))
    bias_up = vector(8, FF // n_f)

    wide = FF // n_f // 2
    w_out = lax.all_gather(out_weight, "fsdp", axis=0, tiled=True)
    up_sent = lax.dynamic_index_in_dim(
        up_weight.reshape(share, n_f, 2, wide), core, 2, keepdims=False
    ).reshape(share, n_f * wide)
    w_up = lax.all_gather(up_sent, "fsdp", axis=0, tiled=True)
    down_sent = lax.dynamic_slice_in_dim(down_weight, core * wide, wide, axis=0)
    w_down = lax.all_gather(down_sent, "fsdp", axis=0, tiled=True)
    w_qkv = lax.all_gather(qkv_weight, "fsdp", axis=0, tiled=True)
    bias_up = lax.dynamic_index_in_dim(bias_up.reshape(n_f, 2, wide), core, 1, False).reshape(-1)

    cot = cotangent[0]
    cot_both = gather(cot[None], "ctx", [1])

    unit_row, _ = standard(row_tokens.astype(F32))
    normed = (unit_row * gain_one + shift_one).astype(BF)
    qkv_f = jnp.dot(normed, w_own, preferred_element_type=F32)
    bq = lax.dynamic_slice_in_dim(bias_query, zi * GW, GW)
    bv = lax.dynamic_slice_in_dim(bias_value, zi * GW, GW)
    q = ((qkv_f[:, :GW] + bq) * (HEAD_DIM**-0.5 * LOG2E)).astype(BF)
    kv = jnp.concatenate([qkv_f[:, GW : 2 * GW], qkv_f[:, 2 * GW :] + bv], axis=1).astype(BF)
    kv_all = gather(kv[None], "ctx", r_masks)
    n_row = GROUPS * rows
    key_seg = jnp.concatenate(
        [segs_of(r ^ (k * ring)) for r in orders(r_masks) for k in range(GROUPS)]
    )
    row_seg = jnp.concatenate([segs_of(k * ring) for k in range(GROUPS)])
    keys = kv_all[:, :, :GW].reshape(-1, GW)
    values = kv_all[:, :, GW:].reshape(-1, GW)
    lane = lax.broadcasted_iota(jnp.int32, (1, HEAD_DIM), 1)
    mark = jnp.where(lane < 8, (key_seg[:, None] == lane), lane < 11).astype(BF)
    seg_row = row_seg.astype(F32)[None]

    attn_ft, attn_row, log_total = forward_attention(q, keys, values, mark, seg_row)

    attn_blocks = attn_row.reshape(GROUPS, rows, GW)
    got = jnp.stack([attn_blocks[0]] + [swap(attn_blocks[k], "ctx", k * ring) for k in range(1, GROUPS)])
    attn = arranged(got, list(range(GROUPS)), zi)
    attn = jnp.swapaxes(attn, 0, 1).reshape(rows, D)

    layer_in = tokens[0].astype(F32)
    mid = layer_in + jnp.dot(attn, w_out, preferred_element_type=F32) + bias_out
    unit_two, scale_two = standard(mid)
    normed_two = (unit_two * gain_two + shift_two).astype(BF)

    both = gather(normed_two[None], "ctx", [1]).reshape(2 * rows, D)
    up_pre = jnp.dot(both, w_up, preferred_element_type=F32) + bias_up
    hidden_f, gelu_back = jax.vjp(gelu_tanh, up_pre)
    hidden = hidden_f.astype(BF)
    cot_flat = cot_both.reshape(2 * rows, D)
    d_up = gelu_back(cols_product(cot_flat, w_down))[0]
    d_up_low = d_up.astype(BF)
    d_normed_part = cols_product(d_up_low, w_up)
    d_normed_two = d_normed_part[:rows] + swap(d_normed_part[rows:].astype(BF), "ctx", 1).astype(F32)
    out_part = jnp.dot(hidden, w_down, preferred_element_type=F32)
    out_stream = (
        mid + out_part[:rows] + swap(out_part[rows:].astype(BF), "ctx", 1).astype(F32) + bias_down
    )

    grad_stream = cot.astype(F32)
    d_gain_two = jnp.sum(d_normed_two * unit_two, axis=0)
    d_shift_two = jnp.sum(d_normed_two, axis=0)
    d_mid = grad_stream + standard_back(d_normed_two * gain_two, unit_two, scale_two)
    d_mid_low = d_mid.astype(BF)
    g_attn = cols_product(d_mid_low, w_out).astype(BF)
    g_blocks = arranged(jnp.swapaxes(g_attn.reshape(rows, GROUPS, GW), 0, 1), list(range(GROUPS)), zi)
    g_row = jnp.stack([g_blocks[0]] + [swap(g_blocks[k], "ctx", k * ring) for k in range(1, GROUPS)])
    g_row = g_row.reshape(n_row, GW)

    d_down_w = rows_product(hidden, cot_flat).astype(BF).reshape(n_f, wide, D)
    d_up_w = rows_product(both, d_up_low).astype(BF)
    d_up_w = jnp.concatenate(
        [d_up_w[:, j * wide : (j + 1) * wide].reshape(n_f, share, wide) for j in range(n_f)], axis=1
    )
    d_out_w = rows_product(attn, d_mid_low).astype(BF)
    same_core = [[i for i in range(n_ctx) if i % 2 == c] for c in range(2)]
    pairs = [[i, i + 1] for i in range(0, n_ctx, 2)]

    def summed(part, groups):
        part = lax.psum_scatter(part, "fsdp", scatter_dimension=0, tiled=False)
        return lax.psum(part, "ctx", axis_index_groups=groups)

    g_out_w = summed(d_out_w.reshape(n_f, share, D), None).astype(F32)
    g_down_w = lax.all_gather(summed(d_down_w, same_core), "ctx", axis_index_groups=pairs)
    g_down_w = g_down_w.reshape(-1, D).astype(F32)
    g_up_w = lax.all_gather(summed(d_up_w, same_core), "ctx", axis_index_groups=pairs)
    g_up_w = jnp.concatenate(
        [g_up_w[c, j * share : (j + 1) * share] for j in range(n_f) for c in range(2)], axis=1
    ).astype(F32)

    valid = (segments[0] > 0).astype(F32)[:, None]
    counts = jnp.stack(
        [
            jnp.sum(valid * layer_in * layer_in),
            jnp.sum(valid * mid * mid),
            jnp.sum(valid * out_stream * out_stream),
            jnp.sum(valid),
        ]
    )
    d_up_bias = jnp.sum(d_up, axis=0).reshape(n_f, 1, wide)
    d_up_bias = jnp.where(
        lax.broadcasted_iota(jnp.int32, (1, 2, 1), 1) == core, d_up_bias, 0.0
    ).reshape(-1, D)
    sums = jnp.concatenate(
        [
            jnp.stack(
                [
                    d_gain_two,
                    d_shift_two,
                    jnp.sum(d_mid, axis=0),
                    jnp.sum(grad_stream, axis=0),
                    jnp.pad(counts, (0, D - 4)),
                ]
            ),
            d_up_bias,
        ],
        axis=0,
    )
    d_q, d_k, d_v, d_bias_q = backward_attention(
        q, g_row, attn_ft, log_total, seg_row, keys, values, mark
    )
    d_kv = jnp.concatenate([d_k, d_v], axis=1).reshape(-1, n_row, 2 * GW)
    d_kv = reduce_blocks(d_kv, "ctx", r_masks)[0]
    d_bias_v = jnp.sum(d_kv[:, GW:].astype(F32), axis=0)
    d_qkv = jnp.concatenate([d_q, d_kv], axis=1)

    d_blocks = d_qkv.reshape(GROUPS, rows, 3 * GW)
    d_got = jnp.stack([d_blocks[0]] + [swap(d_blocks[k], "ctx", k * ring) for k in range(1, GROUPS)])
    d_got = arranged(d_got, list(range(GROUPS)), zi)
    d_own = jnp.concatenate(
        [d_got[g][:, p * GW : (p + 1) * GW] for p in range(3) for g in range(GROUPS)], axis=1
    )
    d_normed = cols_product(d_own, w_qkv)
    unit_one, scale_one = standard(layer_in)
    d_in = d_mid + standard_back(d_normed * gain_one, unit_one, scale_one)

    d_own_w = rows_product(normed, d_qkv).astype(BF)
    d_normed_row = cols_product(d_qkv, w_own)
    wide_q = jnp.zeros((GROUPS, GW), F32)
    group = lax.broadcasted_iota(jnp.int32, (GROUPS, 1), 0) == zi
    last = jnp.stack(
        [
            jnp.sum(d_normed_row * unit_row, axis=0),
            jnp.sum(d_normed_row, axis=0),
            jnp.where(group, d_bias_q, wide_q).reshape(-1),
            jnp.where(group, d_bias_v[None], wide_q).reshape(-1),
        ]
    )
    both_sums = lax.psum(jnp.concatenate([sums, last]), ("ctx", "fsdp"))
    sums, last = both_sums[: sums.shape[0]], both_sums[sums.shape[0] :]
    same_group = [[g * ring + r for r in range(ring)] for g in range(GROUPS)]
    same_place = [[g * ring + r for g in range(GROUPS)] for r in range(ring)]
    pieces = summed(d_own_w.reshape(n_f, share, 3 * GW), same_group)
    pieces = lax.all_gather(pieces, "ctx", axis_index_groups=same_place)
    g_qkv_w = jnp.concatenate(
        [pieces[g, :, q * GW : (q + 1) * GW] for q in range(3) for g in range(GROUPS)], axis=1
    ).astype(F32)

    def own(vec):
        return lax.dynamic_index_in_dim(vec.reshape(n_f, -1), xi, 0, keepdims=False)

    totals = sums[4, :4]
    return (
        out_stream.astype(BF)[None],
        d_in.astype(BF)[None],
        own(last[0]),
        own(last[1]),
        g_qkv_w,
        own(last[2]),
        own(last[3]),
        g_out_w,
        own(sums[2]),
        own(sums[0]),
        own(sums[1]),
        g_up_w,
        own(sums[5:]),
        g_down_w,
        own(sums[3]),
        jnp.sqrt(totals[:3] / (totals[3] * D)),
    )


def solution(mesh):
    token, vec, mat = P("fsdp", "ctx", None), P("fsdp"), P("fsdp", None)
    return jax.shard_map(
        body,
        mesh=mesh,
        in_specs=(
            token, P("fsdp", "ctx"), token, vec, vec, mat, vec, vec, mat, vec, vec, vec, mat, vec,
            mat, vec,
        ),
        out_specs=(
            token, token, vec, vec, mat, vec, vec, mat, vec, vec, vec, mat, vec, mat, vec, P(),
        ),
        check_vma=False,
    )
```
